32 devices in a mesh: freq: 2 (over y), blk: 8 (over z, x), line: 2 (over core).
Axes of the slice: x: 2, y: 2, z: 4, core: 2. Of those that a mesh axis runs over, the one named last changes fastest.
Arguments:
- base_state: float32 [2, 5, 512, 16, 256], P(None, None, ('freq', 'blk'), None, 'line'), parts along dimension 2, may hold values from -6 to 6
- gust_source: float32 [2, 5, 512, 16, 256], P(None, None, ('freq', 'blk'), None, 'line'), parts along dimension 2, may hold values from -6 to 6
- frequency: float32 [2], P('freq'), parts along dimension 0, may hold values from 0.5 to 3
- jacobians: float32 [8, 3, 5, 5], P('blk'), may hold values from -2.5 to 2.5
- dissipation: float32 [256, 16, 256], P('blk', None, 'line'), may hold values from 0.01 to 0.08
- time_step: float32 [256, 16, 256], P('blk', None, 'line'), may hold values from 0.1 to 1
- line_inverse: float32 [16, 256, 256], replicated, may hold values from 0 to 1
- orientation: int32 [8, 2], P('blk'), may hold values from 0 to 1, as said below
Outputs:
- section_state: float32 [2, 5, 512, 16, 256], P(None, None, ('freq', 'blk'), None, 'line'), parts along dimension 2
- smoothed_residual: float32 [2, 5, 512, 16, 256], P(None, None, ('freq', 'blk'), None, 'line'), parts along dimension 2
The draws below stay inside these ranges and needn't reach their ends.
There are 2 independent parts, one for each index of `freq`. The reference program is written for one: setup_inputs(seed, part) draws one part's arguments, and reference() takes and returns one part's arrays. A program takes and returns all parts, laid end to end along the dimension named above; an argument that names none is the same for every part. Nothing has to cross between parts.
Inputs may be any that keep to these rules, and one draw needn't show every extreme that they name: `orientation`: entry [b, 1] equals entry [(b + 1) mod 8, 0]: both describe the same face.
All inputs are finite; a program needn't handle non-finite values.
Results may differ from the reference program's by a relative error of at most 0.0003.
Values sent between devices are 32-bit elements; how exact they have to be, the bound alone decides.
A program may use at most 128 MiB of HBM per device.

```python
import math
import jax
import jax.numpy as jnp
from jax import lax

LINE = 256
J = 16
KL = 32
NVAR = 5
NBLK = 8
NK = 256


def draw_gust_source(key, part):
    shape = (2, NVAR, NK, J, LINE)
    return jax.random.truncated_normal(key, -6.0, 6.0, shape, jnp.float32)


def draw_line_inverse(key, part):
    first, second = jax.random.split(key)
    gaps = jnp.exp(jax.random.uniform(first, (J, 1, 1), jnp.float32, math.log(0.004), math.log(0.3)))
    ratio = 1.0 - gaps
    row_index = lax.broadcasted_iota(jnp.int32, (J, LINE, LINE), 1)
    col_index = lax.broadcasted_iota(jnp.int32, (J, LINE, LINE), 2)
    distance = jnp.abs(row_index - col_index)
    distance = jnp.minimum(distance, LINE - distance).astype(jnp.float32)
    noise = jax.random.uniform(second, (J, LINE, LINE), jnp.float32, -1.0, 1.0)
    weights = jnp.exp(distance * jnp.log(ratio)) * (1.0 + 0.5 * noise)
    centre = 0.5 + 3.0 * ratio / gaps
    return jnp.where(distance == 0.0, 1.0, weights / centre)


def draw_orientation(key, part):
    turnings = jax.random.randint(key, (NBLK,), 0, 2).astype(jnp.int32)
    turnings = turnings.at[0].set(1).at[1].set(0)
    return jnp.stack([jnp.roll(turnings, 1), turnings], axis=1)


def shard_levels(stream_key, extent, pieces, smallest, top_value):
    level = 1.0
    for axis_at, blocks in pieces:
        draws = jax.random.uniform(jax.random.fold_in(jax.random.fold_in(stream_key, 6), axis_at), (blocks,), jnp.float32, smallest / len(pieces), top_value / len(pieces))
        level = level * jnp.repeat(jnp.exp(draws), extent[axis_at] // blocks).reshape((-1,) + (1,) * (len(extent) - 1 - axis_at))
    return level


def centred(stream_key, extent, width, most, cuts=(), held_as=jnp.bfloat16):
    values = width * jax.random.normal(stream_key, extent, jnp.float32)
    if cuts:
        values = values * shard_levels(stream_key, extent, cuts, -0.22, 0.18)
    return jnp.clip(values, -most, most).astype(held_as)


def setup_inputs(seed: int = 0, part: int = 0) -> dict:
    keys = jax.random.split(jax.random.key(seed), 9)
    part_splits = jax.random.split(jax.random.fold_in(keys[8], part), 9)
    base_state = centred(part_splits[0], (2, NVAR, NK, J, LINE), 1.0, 6.0, ((2, 8), (4, 2)), jnp.float32)
    gust_source = draw_gust_source(jax.random.fold_in(jax.random.fold_in(keys[8], part), 71), part)
    frequency = jnp.clip(jax.random.uniform(part_splits[2], (1,), jnp.float32, 0.5, 3.0), 0.5, 3.0)
    jacobians = centred(keys[3], (NBLK, 3, NVAR, NVAR), NVAR ** -0.5, 2.5, ((0, 8),), jnp.float32)
    dissipation = jnp.clip(jnp.exp(math.log(0.08) - 2.0794415 * jax.random.uniform(keys[4], (NK, J, LINE), jnp.float32) ** shard_levels(keys[4], (NK, J, LINE), ((0, 8), (2, 2)), -0.2, 0.2)), 0.01, 0.08)
    time_step = jnp.clip(jnp.exp(math.log(1.0) - 2.3025851 * jax.random.uniform(keys[5], (NK, J, LINE), jnp.float32) ** shard_levels(keys[5], (NK, J, LINE), ((0, 8), (2, 2)), -0.2, 0.2)), 0.1, 1.0)
    line_inverse = draw_line_inverse(jax.random.fold_in(keys[8], 71), part)
    orientation = draw_orientation(jax.random.fold_in(keys[8], 71), part)
    return dict(base_state=base_state, gust_source=gust_source, frequency=frequency, jacobians=jacobians, dissipation=dissipation, time_step=time_step, line_inverse=line_inverse, orientation=orientation)


highest = lax.Precision.HIGHEST
section_coefficient = 0.25


def reorient(planes, facing):
    variable_index = lax.broadcasted_iota(jnp.int32, (1, planes.shape[1], 1, 1, 1), 1)
    sign_row = jnp.where(variable_index == 2, -1.0, 1.0).astype(planes.dtype)
    turned = planes[:, :, :, ::-1, :] * sign_row
    return jnp.where(facing == 1, turned, planes)


def direction_terms(padded, dimension, length, jacobian, damping):
    def shifted(offset):
        return lax.slice_in_dim(padded, offset, offset + length, axis=dimension)
    back_two, back_one, centre, ahead_one, ahead_two = shifted(0), shifted(1), shifted(2), shifted(3), shifted(4)
    central = 0.5 * (ahead_one - back_one)
    convected = jnp.einsum("vw,cwkja->cvkja", jacobian, central, precision=highest)
    fourth = ahead_two - 4.0 * ahead_one + 6.0 * centre - 4.0 * back_one + back_two
    return convected + damping * fourth


def section_residual(fields, kpadded, ipadded, jacobian, damping, source, omega_value):
    jpadded = jnp.pad(fields, ((0, 0), (0, 0), (0, 0), (2, 2), (0, 0)))
    summed = direction_terms(ipadded, 4, fields.shape[4], jacobian[0], damping)
    summed = summed + direction_terms(jpadded, 3, fields.shape[3], jacobian[1], damping)
    summed = summed + direction_terms(kpadded, 2, fields.shape[2], jacobian[2], damping)
    rotated = jnp.stack([-omega_value * fields[1], omega_value * fields[0]])
    return summed + rotated - source


def reference(base_state, gust_source, frequency, jacobians, dissipation, time_step, line_inverse, orientation):
    def split_blocks(array):
        shaped = array.reshape(array.shape[0], array.shape[1], NBLK, KL, array.shape[3], array.shape[4])
        return jnp.moveaxis(shaped, 2, 0)

    fields_all = split_blocks(base_state)
    sources_all = split_blocks(gust_source)
    damping_all = dissipation.reshape(NBLK, KL, J, LINE)
    steps_all = time_step.reshape(NBLK, KL, J, LINE)
    below_all = jnp.roll(fields_all[:, :, :, KL - 2:], 1, axis=0)
    above_all = jnp.roll(fields_all[:, :, :, :2], -1, axis=0)
    omega_value = frequency[0]

    def one_block(items):
        fields, source, below, above, damping, stepping, jacobian, facing = items
        below = reorient(below, facing[0])
        above = reorient(above, facing[1])
        kpadded = jnp.concatenate([below, fields, above], axis=2)
        ipadded = jnp.concatenate([fields[..., LINE - 2:], fields, fields[..., :2]], axis=4)
        residual = section_residual(fields, kpadded, ipadded, jacobian, damping, source, omega_value)
        smoothed = jnp.einsum("jab,cvkjb->cvkja", line_inverse, residual, precision=highest)
        advanced = fields - section_coefficient * stepping * smoothed
        return advanced, smoothed

    advanced_all, smoothed_all = lax.map(one_block, (fields_all, sources_all, below_all, above_all, damping_all, steps_all, jacobians, orientation))

    def join_blocks(array):
        moved = jnp.moveaxis(array, 0, 2)
        return moved.reshape(moved.shape[0], moved.shape[1], NK, J, LINE)

    return join_blocks(advanced_all), join_blocks(smoothed_all)
```

```python
import functools

import jax
import jax.numpy as jnp
from jax import lax
from jax.experimental import pallas as pl
from jax.experimental.pallas import tpu as pltpu
from jax.sharding import PartitionSpec as P

MESH = pl.DeviceIdType.MESH
section_coefficient = 0.25
PAIR = 2


def kernel(
    sizes,
    jac,
    freq,
    facing,
    base,
    gust,
    damp,
    step,
    inverse,
    advanced,
    smoothed,
    ubuf,
    gbuf,
    dbuf,
    tbuf,
    wbuf,
    wcat,
    pack_out,
    pack_in,
    own,
    other,
    turned,
    local_sem,
    halo_send,
    halo_recv,
    pack_send,
    pack_recv,
    res_send,
    res_recv,
):
    nblk, kl, nj, ni, cv = sizes
    nv = cv // 2
    f32, bf16 = jnp.float32, jnp.bfloat16
    blk = lax.axis_index("blk")
    line = lax.axis_index("line")
    right = lax.rem(blk + 1, nblk)
    left = lax.rem(blk + nblk - 1, nblk)
    mate = 1 - line

    loads = [
        pltpu.make_async_copy(
            base, ubuf.at[:, pl.ds(2, kl), pl.ds(8, nj), :], local_sem.at[0]
        ),
        pltpu.make_async_copy(
            inverse.at[:, pl.ds(pl.multiple_of(line * ni, ni), ni), pl.ds(pl.multiple_of(line * ni, ni), ni)],
            wbuf.at[:, :, pl.ds(0, ni)],
            local_sem.at[1],
        ),
        pltpu.make_async_copy(
            inverse.at[:, pl.ds(pl.multiple_of(line * ni, ni), ni), pl.ds(pl.multiple_of(mate * ni, ni), ni)],
            wbuf.at[:, :, pl.ds(ni, ni)],
            local_sem.at[2],
        ),
        pltpu.make_async_copy(gust, gbuf, local_sem.at[3]),
        pltpu.make_async_copy(damp, dbuf, local_sem.at[4]),
        pltpu.make_async_copy(step, tbuf, local_sem.at[5]),
    ]
    for copy in loads:
        copy.start()

    barrier = pltpu.get_barrier_semaphore()
    pl.semaphore_signal(barrier, inc=1, device_id={"blk": right}, device_id_type=MESH)
    pl.semaphore_signal(barrier, inc=1, device_id={"blk": left}, device_id_type=MESH)
    pl.semaphore_signal(barrier, inc=1, device_id={"line": mate}, device_id_type=MESH)
    pl.semaphore_wait(barrier, 3)

    to_right = pltpu.make_async_remote_copy(
        src_ref=base.at[:, pl.ds(kl - 2, 2)],
        dst_ref=ubuf.at[:, pl.ds(0, 2), pl.ds(8, nj), :],
        send_sem=halo_send.at[0],
        recv_sem=halo_recv.at[0],
        device_id={"blk": right},
        device_id_type=MESH,
    )
    to_left = pltpu.make_async_remote_copy(
        src_ref=base.at[:, pl.ds(0, 2)],
        dst_ref=ubuf.at[:, pl.ds(kl + 2, 2), pl.ds(8, nj), :],
        send_sem=halo_send.at[1],
        recv_sem=halo_recv.at[1],
        device_id={"blk": left},
        device_id_type=MESH,
    )
    to_right.start()
    to_left.start()

    def clear(k, carry):
        zero = jnp.zeros((cv, 8, ni), f32)
        ubuf[:, k + 2, 0:8, :] = zero
        ubuf[:, k + 2, nj + 8 : nj + 16, :] = zero
        return carry

    lax.fori_loop(0, kl, clear, 0)

    lane = lax.broadcasted_iota(jnp.int32, (nj, ni), 1)
    edge = (lane < 2) | (lane >= ni - 2)

    loads[0].wait()

    def pack(k, carry):
        return tuple(
            carry[n]
            + pltpu.roll(jnp.where(edge, ubuf[n, k + 2, 8 : nj + 8, :], 0.0), 4 * k, 1)
            for n in range(cv)
        )

    packed = lax.fori_loop(
        0, kl, pack, tuple(jnp.zeros((nj, ni), f32) for _ in range(cv))
    )
    for n in range(cv):
        pack_out[n] = packed[n]
    swap = pltpu.make_async_remote_copy(
        src_ref=pack_out,
        dst_ref=pack_in,
        send_sem=pack_send,
        recv_sem=pack_recv,
        device_id={"line": mate},
        device_id_type=MESH,
    )
    swap.start()

    loads[1].wait()
    loads[2].wait()

    def split(j, carry):
        values = wbuf[j]
        high = values.astype(bf16)
        wcat[j, 0:ni, :] = high
        wcat[j, ni : 2 * ni, :] = (values - high.astype(f32)).astype(bf16)
        return carry

    lax.fori_loop(0, nj, split, 0)

    loads[3].wait()
    loads[4].wait()
    loads[5].wait()
    swap.wait()

    omega = freq[0]

    def plane(k):
        damping = dbuf[k]
        shift = lax.rem(ni - 4 * k, ni)
        for c in range(2):
            central = []
            fourth = []
            for v in range(nv):
                n = c * nv + v
                u = ubuf[n, k + 2, 8 : nj + 8, :]
                k1, k2 = ubuf[n, k + 3, 8 : nj + 8, :], ubuf[n, k + 4, 8 : nj + 8, :]
                kb1, kb2 = ubuf[n, k + 1, 8 : nj + 8, :], ubuf[n, k, 8 : nj + 8, :]
                j1, j2 = ubuf[n, k + 2, 9 : nj + 9, :], ubuf[n, k + 2, 10 : nj + 10, :]
                jb1, jb2 = ubuf[n, k + 2, 7 : nj + 7, :], ubuf[n, k + 2, 6 : nj + 6, :]
                h = pltpu.roll(pack_in[n], shift, 1)
                i1 = pltpu.roll(jnp.where(lane == 0, h, u), ni - 1, 1)
                i2 = pltpu.roll(jnp.where(lane < 2, h, u), ni - 2, 1)
                ib1 = pltpu.roll(jnp.where(lane == ni - 1, h, u), 1, 1)
                ib2 = pltpu.roll(jnp.where(lane >= ni - 2, h, u), 2, 1)
                central.append((i1 - ib1, j1 - jb1, k1 - kb1))
                fourth.append(
                    ((k2 + kb2) + (j2 + jb2) + (i2 + ib2))
                    - 4.0 * ((k1 + kb1) + (j1 + jb1) + (i1 + ib1))
                    + 18.0 * u
                )
            for v in range(nv):
                total = damping * fourth[v] - gbuf[c * nv + v, k]
                if c == 0:
                    total = total - omega * ubuf[nv + v, k + 2, 8 : nj + 8, :]
                else:
                    total = total + omega * ubuf[v, k + 2, 8 : nj + 8, :]
                for w in range(nv):
                    for d in range(3):
                        total = total + jac[d * nv * nv + v * nv + w] * central[w][d]
                own[c * nv + v, pl.ds(pl.multiple_of(k * nj, nj), nj), :] = total

    def send(pair):
        rows = pl.ds(pl.multiple_of(pair * (PAIR * nj), PAIR * nj), PAIR * nj)
        return pltpu.make_async_remote_copy(
            src_ref=own.at[:, rows, :],
            dst_ref=other.at[:, rows, :],
            send_sem=res_send.at[pair],
            recv_sem=res_recv.at[pair],
            device_id={"line": mate},
            device_id_type=MESH,
        )

    def work(pair):
        def one(k, carry):
            plane(pair * PAIR + k)
            return carry

        lax.fori_loop(0, PAIR, one, 0)
        send(pair).start()

    pairs = kl // PAIR
    quarter = pairs // 4

    def middle_pair(n):
        return n + quarter

    def outer_pair(n):
        return n + 1 + (n // (quarter - 1)) * (pairs // 2)

    def run_middle(n, carry):
        work(middle_pair(n))
        return carry

    def run_outer(n, carry):
        work(outer_pair(n))
        return carry

    lax.fori_loop(0, pairs // 2, run_middle, 0)
    lax.fori_loop(0, 2 * (quarter - 1), run_outer, 0)

    def product(starts, count):
        def one(j, carry):
            mine, theirs = [], []
            for n in range(cv):
                for k0 in starts:
                    rows = pl.ds(k0 * nj + j, count, stride=nj)
                    mine.append(own[n, rows, :])
                    theirs.append(other[n, rows, :])
            x = jnp.concatenate(
                [jnp.concatenate(mine, axis=0), jnp.concatenate(theirs, axis=0)], axis=1
            )
            high = x.astype(bf16)
            low = (x - high.astype(f32)).astype(bf16)
            weight = wcat[j]
            contract = (((1,), (1,)), ((), ()))
            both = lax.dot_general(high, weight, contract, preferred_element_type=f32)
            rest = lax.dot_general(
                low, weight[0:ni], contract, preferred_element_type=f32
            )
            out = both[:, 0:ni] + (both[:, ni : 2 * ni] + rest)
            at = 0
            for n in range(cv):
                for k0 in starts:
                    smoothed[n, pl.ds(k0 * nj + j, count, stride=nj), :] = out[
                        at : at + count
                    ]
                    at += count
            return carry

        lax.fori_loop(0, nj, one, 0)

    def update(first, number):
        def one(k, carry):
            rows = pl.ds(pl.multiple_of((first + k) * nj, nj), nj)
            scale = section_coefficient * tbuf[first + k]
            for n in range(cv):
                advanced[n, rows, :] = (
                    ubuf[n, first + k + 2, 8 : nj + 8, :] - scale * smoothed[n, rows, :]
                )
            return carry

        lax.fori_loop(0, number, one, 0)

    def arrived(n, carry):
        send(middle_pair(n)).wait_recv()
        return carry

    lax.fori_loop(0, pairs // 2, arrived, 0)
    product([kl // 4], kl // 2)
    update(kl // 4, kl // 2)

    to_right.wait()
    to_left.wait()

    for side, first in ((0, 0), (1, kl + 2)):
        turn = facing[side] == 1
        for p in range(2):
            for n in range(cv):
                turned[n * 2 + p] = ubuf[n, first + p, 8 : nj + 8, :]
        for p in range(2):
            for n in range(cv):
                sign = -1.0 if n % nv == 2 else 1.0
                rows = [turned[n * 2 + p, r : r + 1, :] for r in range(nj - 1, -1, -1)]
                flipped = sign * jnp.concatenate(rows, axis=0)
                ubuf[n, first + p, 8 : nj + 8, :] = jnp.where(
                    turn, flipped, turned[n * 2 + p]
                )

    work(0)
    work(pairs - 1)

    def outer_arrived(n, carry):
        send(outer_pair(n)).wait_recv()
        return carry

    lax.fori_loop(0, 2 * (quarter - 1), outer_arrived, 0)
    send(0).wait_recv()
    send(pairs - 1).wait_recv()
    product([0, kl - kl // 4], kl // 4)
    update(0, kl // 4)
    update(kl - kl // 4, kl // 4)

    def sent(pair, carry):
        send(pair).wait_send()
        return carry

    lax.fori_loop(0, pairs, sent, 0)


def body(
    nblk,
    base_state,
    gust_source,
    frequency,
    jacobians,
    dissipation,
    time_step,
    line_inverse,
    orientation,
):
    nc, nv, kl, nj, ni = base_state.shape
    cv = nc * nv
    f32 = jnp.float32
    pairs = kl // PAIR
    out = pltpu.VMEM((cv, kl * nj, ni), f32)
    smem = pl.BlockSpec(memory_space=pltpu.SMEM)
    hbm = pl.BlockSpec(memory_space=pltpu.HBM)
    vmem = pl.BlockSpec(memory_space=pltpu.VMEM)
    dma = pltpu.SemaphoreType.DMA
    advanced, smoothed = pl.pallas_call(
        functools.partial(kernel, (nblk, kl, nj, ni, cv)),
        out_shape=(out, out),
        in_specs=[smem] * 3 + [hbm] * 5,
        out_specs=(vmem, vmem),
        scratch_shapes=[
            pltpu.VMEM((cv, kl + 4, nj + 16, ni), f32),
            pltpu.VMEM((cv, kl, nj, ni), f32),
            pltpu.VMEM((kl, nj, ni), f32),
            pltpu.VMEM((kl, nj, ni), f32),
            pltpu.VMEM((nj, ni, 2 * ni), f32),
            pltpu.VMEM((nj, 2 * ni, 2 * ni), jnp.bfloat16),
            pltpu.VMEM((cv, nj, ni), f32),
            pltpu.VMEM((cv, nj, ni), f32),
            pltpu.VMEM((cv, kl * nj, ni), f32),
            pltpu.VMEM((cv, kl * nj, ni), f32),
            pltpu.VMEM((cv * 2, nj, ni), f32),
            dma((6,)),
            dma((2,)),
            dma((2,)),
            dma,
            dma,
            dma((pairs,)),
            dma((pairs,)),
        ],
        compiler_params=pltpu.CompilerParams(
            collective_id=0, has_side_effects=True, vmem_limit_bytes=54 * 1024 * 1024
        ),
    )(
        0.5 * jacobians.reshape(-1),
        frequency,
        orientation.reshape(-1),
        base_state.reshape(cv, kl, nj, ni),
        gust_source.reshape(cv, kl, nj, ni),
        dissipation,
        time_step,
        line_inverse,
    )
    return advanced.reshape(base_state.shape), smoothed.reshape(base_state.shape)


def solution(mesh):
    in_specs = (
        P(None, None, ("freq", "blk"), None, "line"),
        P(None, None, ("freq", "blk"), None, "line"),
        P("freq"),
        P("blk", None, None, None),
        P("blk", None, "line"),
        P("blk", None, "line"),
        P(),
        P("blk", None),
    )
    out_specs = (
        P(None, None, ("freq", "blk"), None, "line"),
        P(None, None, ("freq", "blk"), None, "line"),
    )
    return jax.shard_map(
        functools.partial(body, mesh.shape["blk"]),
        mesh=mesh,
        in_specs=in_specs,
        out_specs=out_specs,
        check_vma=False,
    )
```

```python
import functools

import jax
import jax.numpy as jnp
from jax import lax
from jax.experimental import pallas as pl
from jax.experimental.pallas import tpu as pltpu
from jax.sharding import PartitionSpec as P

MESH = pl.DeviceIdType.MESH
section_coefficient = 0.25
PAIR = 2


def kernel(
    sizes,
    jac,
    freq,
    facing,
    base,
    gust,
    damp,
    step,
    inverse,
    advanced,
    smoothed,
    ubuf,
    gbuf,
    dbuf,
    tbuf,
    wbuf,
    wcat,
    pack_out,
    pack_in,
    own,
    other,
    turned,
    local_sem,
    halo_send,
    halo_recv,
    pack_send,
    pack_recv,
    res_send,
    res_recv,
):
    nblk, kl, nj, ni, cv = sizes
    nv = cv // 2
    f32, bf16 = jnp.float32, jnp.bfloat16
    blk = lax.axis_index("blk")
    line = lax.axis_index("line")
    right = lax.rem(blk + 1, nblk)
    left = lax.rem(blk + nblk - 1, nblk)
    mate = 1 - line

    loads = [
        pltpu.make_async_copy(
            base, ubuf.at[:, pl.ds(2, kl), pl.ds(8, nj), :], local_sem.at[0]
        ),
        pltpu.make_async_copy(
            inverse.at[:, pl.ds(pl.multiple_of(line * ni, ni), ni), pl.ds(pl.multiple_of(line * ni, ni), ni)],
            wbuf.at[:, :, pl.ds(0, ni)],
            local_sem.at[1],
        ),
        pltpu.make_async_copy(
            inverse.at[:, pl.ds(pl.multiple_of(line * ni, ni), ni), pl.ds(pl.multiple_of(mate * ni, ni), ni)],
            wbuf.at[:, :, pl.ds(ni, ni)],
            local_sem.at[2],
        ),
        pltpu.make_async_copy(gust, gbuf, local_sem.at[3]),
        pltpu.make_async_copy(damp, dbuf, local_sem.at[4]),
        pltpu.make_async_copy(step, tbuf, local_sem.at[5]),
    ]
    for copy in loads:
        copy.start()

    barrier = pltpu.get_barrier_semaphore()
    pl.semaphore_signal(barrier, inc=1, device_id={"blk": right}, device_id_type=MESH)
    pl.semaphore_signal(barrier, inc=1, device_id={"blk": left}, device_id_type=MESH)
    pl.semaphore_signal(barrier, inc=1, device_id={"line": mate}, device_id_type=MESH)
    pl.semaphore_wait(barrier, 3)

    to_right = pltpu.make_async_remote_copy(
        src_ref=base.at[:, pl.ds(kl - 2, 2)],
        dst_ref=ubuf.at[:, pl.ds(0, 2), pl.ds(8, nj), :],
        send_sem=halo_send.at[0],
        recv_sem=halo_recv.at[0],
        device_id={"blk": right},
        device_id_type=MESH,
    )
    to_left = pltpu.make_async_remote_copy(
        src_ref=base.at[:, pl.ds(0, 2)],
        dst_ref=ubuf.at[:, pl.ds(kl + 2, 2), pl.ds(8, nj), :],
        send_sem=halo_send.at[1],
        recv_sem=halo_recv.at[1],
        device_id={"blk": left},
        device_id_type=MESH,
    )
    to_right.start()
    to_left.start()

    def clear(k, carry):
        zero = jnp.zeros((cv, 8, ni), f32)
        ubuf[:, k + 2, 0:8, :] = zero
        ubuf[:, k + 2, nj + 8 : nj + 16, :] = zero
        return carry

    lax.fori_loop(0, kl, clear, 0)

    lane = lax.broadcasted_iota(jnp.int32, (nj, ni), 1)
    edge = (lane < 2) | (lane >= ni - 2)

    loads[0].wait()

    def pack(k, carry):
        return tuple(
            carry[n]
            + pltpu.roll(jnp.where(edge, ubuf[n, k + 2, 8 : nj + 8, :], 0.0), 4 * k, 1)
            for n in range(cv)
        )

    packed = lax.fori_loop(
        0, kl, pack, tuple(jnp.zeros((nj, ni), f32) for _ in range(cv)), unroll=4
    )
    for n in range(cv):
        pack_out[n] = packed[n]
    swap = pltpu.make_async_remote_copy(
        src_ref=pack_out,
        dst_ref=pack_in,
        send_sem=pack_send,
        recv_sem=pack_recv,
        device_id={"line": mate},
        device_id_type=MESH,
    )
    swap.start()

    loads[1].wait()
    loads[2].wait()

    def split(j, carry):
        values = wbuf[j]
        high = values.astype(bf16)
        wcat[j, 0:ni, :] = high
        wcat[j, ni : 2 * ni, :] = (values - high.astype(f32)).astype(bf16)
        return carry

    lax.fori_loop(0, nj, split, 0, unroll=2)

    loads[3].wait()
    loads[4].wait()
    loads[5].wait()
    swap.wait()

    omega = freq[0]

    def plane(k):
        damping = dbuf[k]
        shift = lax.rem(ni - 4 * k, ni)
        for c in range(2):
            central = []
            fourth = []
            for v in range(nv):
                n = c * nv + v
                u = ubuf[n, k + 2, 8 : nj + 8, :]
                k1, k2 = ubuf[n, k + 3, 8 : nj + 8, :], ubuf[n, k + 4, 8 : nj + 8, :]
                kb1, kb2 = ubuf[n, k + 1, 8 : nj + 8, :], ubuf[n, k, 8 : nj + 8, :]
                j1, j2 = ubuf[n, k + 2, 9 : nj + 9, :], ubuf[n, k + 2, 10 : nj + 10, :]
                jb1, jb2 = ubuf[n, k + 2, 7 : nj + 7, :], ubuf[n, k + 2, 6 : nj + 6, :]
                h = pltpu.roll(pack_in[n], shift, 1)
                i1 = pltpu.roll(jnp.where(lane == 0, h, u), ni - 1, 1)
                i2 = pltpu.roll(jnp.where(lane < 2, h, u), ni - 2, 1)
                ib1 = pltpu.roll(jnp.where(lane == ni - 1, h, u), 1, 1)
                ib2 = pltpu.roll(jnp.where(lane >= ni - 2, h, u), 2, 1)
                central.append((i1 - ib1, j1 - jb1, k1 - kb1))
                fourth.append(
                    ((k2 + kb2) + (j2 + jb2) + (i2 + ib2))
                    - 4.0 * ((k1 + kb1) + (j1 + jb1) + (i1 + ib1))
                    + 18.0 * u
                )
            for v in range(nv):
                flux = jnp.zeros((nj, ni), f32)
                for w in range(nv):
                    for d in range(3):
                        flux = flux + jac[d, v, w] * central[w][d]
                total = damping * fourth[v] - gbuf[c * nv + v, k] + 0.5 * flux
                if c == 0:
                    total = total - omega * ubuf[nv + v, k + 2, 8 : nj + 8, :]
                else:
                    total = total + omega * ubuf[v, k + 2, 8 : nj + 8, :]
                own[c * nv + v, pl.ds(pl.multiple_of(k * nj, nj), nj), :] = total

    def send(pair):
        rows = pl.ds(pl.multiple_of(pair * (PAIR * nj), PAIR * nj), PAIR * nj)
        return pltpu.make_async_remote_copy(
            src_ref=own.at[:, rows, :],
            dst_ref=other.at[:, rows, :],
            send_sem=res_send.at[pair],
            recv_sem=res_recv.at[pair],
            device_id={"line": mate},
            device_id_type=MESH,
        )

    def work(pair):
        def one(k, carry):
            plane(pair * PAIR + k)
            return carry

        lax.fori_loop(0, PAIR, one, 0)
        send(pair).start()

    pairs = kl // PAIR
    quarter = pairs // 4

    def middle_pair(n):
        return n + quarter

    def outer_pair(n):
        return n + 1 + (n // (quarter - 1)) * (pairs // 2)

    def run_middle(n, carry):
        work(middle_pair(n))
        return carry

    def run_outer(n, carry):
        work(outer_pair(n))
        return carry

    lax.fori_loop(0, pairs // 2, run_middle, 0)
    lax.fori_loop(0, 2 * (quarter - 1), run_outer, 0)

    def product(starts, count):
        def one(j, carry):
            mine, theirs = [], []
            for n in range(cv):
                for k0 in starts:
                    rows = pl.ds(k0 * nj + j, count, stride=nj)
                    mine.append(own[n, rows, :])
                    theirs.append(other[n, rows, :])
            x = jnp.concatenate(
                [jnp.concatenate(mine, axis=0), jnp.concatenate(theirs, axis=0)], axis=1
            )
            high = x.astype(bf16)
            low = (x - high.astype(f32)).astype(bf16)
            weight = wcat[j]
            contract = (((1,), (1,)), ((), ()))
            both = lax.dot_general(high, weight, contract, preferred_element_type=f32)
            rest = lax.dot_general(
                low, weight[0:ni], contract, preferred_element_type=f32
            )
            out = both[:, 0:ni] + (both[:, ni : 2 * ni] + rest)
            at = 0
            for n in range(cv):
                for k0 in starts:
                    smoothed[n, pl.ds(k0 * nj + j, count, stride=nj), :] = out[
                        at : at + count
                    ]
                    at += count
            return carry

        lax.fori_loop(0, nj, one, 0, unroll=8)

    def update(first, number):
        def one(k, carry):
            rows = pl.ds(pl.multiple_of((first + k) * nj, nj), nj)
            scale = section_coefficient * tbuf[first + k]
            for n in range(cv):
                advanced[n, rows, :] = (
                    ubuf[n, first + k + 2, 8 : nj + 8, :] - scale * smoothed[n, rows, :]
                )
            return carry

        lax.fori_loop(0, number, one, 0, unroll=2)

    def arrived(n, carry):
        send(middle_pair(n)).wait_recv()
        return carry

    lax.fori_loop(0, pairs // 2, arrived, 0)
    product([kl // 4], kl // 2)
    update(kl // 4, kl // 2)

    to_right.wait()
    to_left.wait()

    for side, first in ((0, 0), (1, kl + 2)):
        turn = facing[side] == 1
        for p in range(2):
            for n in range(cv):
                at = (p * cv + n) * nj
                turned[0, at : at + nj, :] = ubuf[n, first + p, 8 : nj + 8, :]
        for j in range(nj):
            turned[1, pl.ds(j, 2 * cv, stride=nj), :] = turned[
                0, pl.ds(nj - 1 - j, 2 * cv, stride=nj), :
            ]
        for p in range(2):
            for n in range(cv):
                sign = -1.0 if n % nv == 2 else 1.0
                at = (p * cv + n) * nj
                ubuf[n, first + p, 8 : nj + 8, :] = jnp.where(
                    turn, sign * turned[1, at : at + nj, :], turned[0, at : at + nj, :]
                )

    work(0)
    work(pairs - 1)

    def outer_arrived(n, carry):
        send(outer_pair(n)).wait_recv()
        return carry

    lax.fori_loop(0, 2 * (quarter - 1), outer_arrived, 0)
    send(0).wait_recv()
    send(pairs - 1).wait_recv()
    product([0, kl - kl // 4], kl // 4)
    update(0, kl // 4)
    update(kl - kl // 4, kl // 4)

    def sent(pair, carry):
        send(pair).wait_send()
        return carry

    lax.fori_loop(0, pairs, sent, 0)


def body(
    nblk,
    base_state,
    gust_source,
    frequency,
    jacobians,
    dissipation,
    time_step,
    line_inverse,
    orientation,
):
    nc, nv, kl, nj, ni = base_state.shape
    cv = nc * nv
    f32 = jnp.float32
    pairs = kl // PAIR
    out = pltpu.VMEM((cv, kl * nj, ni), f32)
    smem = pl.BlockSpec(memory_space=pltpu.SMEM)
    hbm = pl.BlockSpec(memory_space=pltpu.HBM)
    vmem = pl.BlockSpec(memory_space=pltpu.VMEM)
    dma = pltpu.SemaphoreType.DMA
    advanced, smoothed = pl.pallas_call(
        functools.partial(kernel, (nblk, kl, nj, ni, cv)),
        out_shape=(out, out),
        in_specs=[smem] * 3 + [hbm] * 5,
        out_specs=(vmem, vmem),
        scratch_shapes=[
            pltpu.VMEM((cv, kl + 4, nj + 16, ni), f32),
            pltpu.VMEM((cv, kl, nj, ni), f32),
            pltpu.VMEM((kl, nj, ni), f32),
            pltpu.VMEM((kl, nj, ni), f32),
            pltpu.VMEM((nj, ni, 2 * ni), f32),
            pltpu.VMEM((nj, 2 * ni, 2 * ni), jnp.bfloat16),
            pltpu.VMEM((cv, nj, ni), f32),
            pltpu.VMEM((cv, nj, ni), f32),
            pltpu.VMEM((cv, kl * nj, ni), f32),
            pltpu.VMEM((cv, kl * nj, ni), f32),
            pltpu.VMEM((2, cv * 2 * nj, ni), f32),
            dma((6,)),
            dma((2,)),
            dma((2,)),
            dma,
            dma,
            dma((pairs,)),
            dma((pairs,)),
        ],
        compiler_params=pltpu.CompilerParams(
            collective_id=0, has_side_effects=True, vmem_limit_bytes=54 * 1024 * 1024
        ),
    )(
        jacobians.reshape(jacobians.shape[1:]),
        frequency,
        orientation.reshape(-1),
        base_state.reshape(cv, kl, nj, ni),
        gust_source.reshape(cv, kl, nj, ni),
        dissipation,
        time_step,
        line_inverse,
    )
    return advanced.reshape(base_state.shape), smoothed.reshape(base_state.shape)


def solution(mesh):
    in_specs = (
        P(None, None, ("freq", "blk"), None, "line"),
        P(None, None, ("freq", "blk"), None, "line"),
        P("freq"),
        P("blk", None, None, None),
        P("blk", None, "line"),
        P("blk", None, "line"),
        P(),
        P("blk", None),
    )
    out_specs = (
        P(None, None, ("freq", "blk"), None, "line"),
        P(None, None, ("freq", "blk"), None, "line"),
    )
    return jax.shard_map(
        functools.partial(body, mesh.shape["blk"]),
        mesh=mesh,
        in_specs=in_specs,
        out_specs=out_specs,
        check_vma=False,
    )
```

```python
import functools

import jax
import jax.numpy as jnp
from jax import lax
from jax.experimental import pallas as pl
from jax.experimental.pallas import tpu as pltpu
from jax.sharding import PartitionSpec as P

MESH = pl.DeviceIdType.MESH
section_coefficient = 0.25
PAIR = 2
MIXED = 4


def kernel(
    sizes,
    jac,
    freq,
    facing,
    base,
    gust,
    damp,
    step,
    inverse,
    advanced,
    smoothed,
    ubuf,
    gbuf,
    dbuf,
    tbuf,
    wbuf,
    wcat,
    pack_out,
    pack_in,
    own,
    other,
    turned,
    local_sem,
    halo_send,
    halo_recv,
    pack_send,
    pack_recv,
    res_send,
    res_recv,
):
    nblk, kl, nj, ni, cv = sizes
    nv = cv // 2
    f32, bf16 = jnp.float32, jnp.bfloat16
    blk = lax.axis_index("blk")
    line = lax.axis_index("line")
    right = lax.rem(blk + 1, nblk)
    left = lax.rem(blk + nblk - 1, nblk)
    mate = 1 - line

    loads = [
        pltpu.make_async_copy(
            base, ubuf.at[:, pl.ds(2, kl), pl.ds(8, nj), :], local_sem.at[0]
        ),
        pltpu.make_async_copy(
            inverse.at[:, pl.ds(pl.multiple_of(line * ni, ni), ni), pl.ds(pl.multiple_of(line * ni, ni), ni)],
            wbuf.at[:, :, pl.ds(0, ni)],
            local_sem.at[1],
        ),
        pltpu.make_async_copy(
            inverse.at[:, pl.ds(pl.multiple_of(line * ni, ni), ni), pl.ds(pl.multiple_of(mate * ni, ni), ni)],
            wbuf.at[:, :, pl.ds(ni, ni)],
            local_sem.at[2],
        ),
        pltpu.make_async_copy(gust, gbuf, local_sem.at[3]),
        pltpu.make_async_copy(damp, dbuf, local_sem.at[4]),
        pltpu.make_async_copy(step, tbuf, local_sem.at[5]),
    ]
    for copy in loads:
        copy.start()

    barrier = pltpu.get_barrier_semaphore()
    pl.semaphore_signal(barrier, inc=1, device_id={"blk": right}, device_id_type=MESH)
    pl.semaphore_signal(barrier, inc=1, device_id={"blk": left}, device_id_type=MESH)
    pl.semaphore_signal(barrier, inc=1, device_id={"line": mate}, device_id_type=MESH)
    pl.semaphore_wait(barrier, 3)

    to_right = pltpu.make_async_remote_copy(
        src_ref=base.at[:, pl.ds(kl - 2, 2)],
        dst_ref=ubuf.at[:, pl.ds(0, 2), pl.ds(8, nj), :],
        send_sem=halo_send.at[0],
        recv_sem=halo_recv.at[0],
        device_id={"blk": right},
        device_id_type=MESH,
    )
    to_left = pltpu.make_async_remote_copy(
        src_ref=base.at[:, pl.ds(0, 2)],
        dst_ref=ubuf.at[:, pl.ds(kl + 2, 2), pl.ds(8, nj), :],
        send_sem=halo_send.at[1],
        recv_sem=halo_recv.at[1],
        device_id={"blk": left},
        device_id_type=MESH,
    )
    to_right.start()
    to_left.start()

    def clear(k, carry):
        zero = jnp.zeros((cv, 8, ni), f32)
        ubuf[:, k + 2, 0:8, :] = zero
        ubuf[:, k + 2, nj + 8 : nj + 16, :] = zero
        return carry

    lax.fori_loop(0, kl, clear, 0)

    lane = lax.broadcasted_iota(jnp.int32, (nj, ni), 1)
    edge = (lane < 2) | (lane >= ni - 2)

    loads[0].wait()

    def pack(k, carry):
        return tuple(
            carry[n]
            + pltpu.roll(jnp.where(edge, ubuf[n, k + 2, 8 : nj + 8, :], 0.0), 4 * k, 1)
            for n in range(cv)
        )

    packed = lax.fori_loop(
        0, kl, pack, tuple(jnp.zeros((nj, ni), f32) for _ in range(cv)), unroll=4
    )
    for n in range(cv):
        pack_out[n] = packed[n]
    swap = pltpu.make_async_remote_copy(
        src_ref=pack_out,
        dst_ref=pack_in,
        send_sem=pack_send,
        recv_sem=pack_recv,
        device_id={"line": mate},
        device_id_type=MESH,
    )
    swap.start()

    loads[1].wait()
    loads[2].wait()

    def split(j, carry):
        values = wbuf[j]
        high = values.astype(bf16)
        wcat[j, 0:ni, :] = high
        wcat[j, ni : 2 * ni, :] = (values - high.astype(f32)).astype(bf16)
        return carry

    lax.fori_loop(0, nj, split, 0, unroll=2)

    loads[3].wait()
    loads[4].wait()
    loads[5].wait()
    swap.wait()

    omega = freq[0]

    def plane(k):
        damping = dbuf[k]
        shift = lax.rem(ni - 4 * k, ni)
        for c in range(2):
            central = []
            fourth = []
            for v in range(nv):
                n = c * nv + v
                u = ubuf[n, k + 2, 8 : nj + 8, :]
                k1, k2 = ubuf[n, k + 3, 8 : nj + 8, :], ubuf[n, k + 4, 8 : nj + 8, :]
                kb1, kb2 = ubuf[n, k + 1, 8 : nj + 8, :], ubuf[n, k, 8 : nj + 8, :]
                j1, j2 = ubuf[n, k + 2, 9 : nj + 9, :], ubuf[n, k + 2, 10 : nj + 10, :]
                jb1, jb2 = ubuf[n, k + 2, 7 : nj + 7, :], ubuf[n, k + 2, 6 : nj + 6, :]
                h = pltpu.roll(pack_in[n], shift, 1)
                i1 = pltpu.roll(jnp.where(lane == 0, h, u), ni - 1, 1)
                i2 = pltpu.roll(jnp.where(lane < 2, h, u), ni - 2, 1)
                ib1 = pltpu.roll(jnp.where(lane == ni - 1, h, u), 1, 1)
                ib2 = pltpu.roll(jnp.where(lane >= ni - 2, h, u), 2, 1)
                central.append((i1 - ib1, j1 - jb1, k1 - kb1))
                fourth.append(
                    ((k2 + kb2) + (j2 + jb2) + (i2 + ib2))
                    - 4.0 * ((k1 + kb1) + (j1 + jb1) + (i1 + ib1))
                    + 18.0 * u
                )
            for v in range(nv):
                flux = jnp.zeros((nj, ni), f32)
                for w in range(nv):
                    for d in range(3):
                        flux = flux + jac[d, v, w] * central[w][d]
                total = damping * fourth[v] - gbuf[c * nv + v, k] + 0.5 * flux
                if c == 0:
                    total = total - omega * ubuf[nv + v, k + 2, 8 : nj + 8, :]
                else:
                    total = total + omega * ubuf[v, k + 2, 8 : nj + 8, :]
                own[c * nv + v, pl.ds(pl.multiple_of(k * nj, nj), nj), :] = total

    def send(pair):
        rows = pl.ds(pl.multiple_of(pair * (PAIR * nj), PAIR * nj), PAIR * nj)
        return pltpu.make_async_remote_copy(
            src_ref=own.at[:, rows, :],
            dst_ref=other.at[:, rows, :],
            send_sem=res_send.at[pair],
            recv_sem=res_recv.at[pair],
            device_id={"line": mate},
            device_id_type=MESH,
        )

    def work(pair):
        def one(k, carry):
            plane(pair * PAIR + k)
            return carry

        lax.fori_loop(0, PAIR, one, 0)
        send(pair).start()

    pairs = kl // PAIR
    quarter = pairs // 4

    def middle_pair(n):
        return n + quarter

    def outer_pair(n):
        return n + 1 + (n // (quarter - 1)) * (pairs // 2)

    def run_middle(n, carry):
        work(middle_pair(n))
        return carry

    def run_outer(n, carry):
        work(outer_pair(n))
        return carry

    lax.fori_loop(0, pairs // 2, run_middle, 0)
    lax.fori_loop(0, 2 * (quarter - 1) - MIXED, run_outer, 0)

    def row_product(starts, count):
        def row(j):
            mine, theirs = [], []
            for n in range(cv):
                for k0 in starts:
                    rows = pl.ds(k0 * nj + j, count, stride=nj)
                    mine.append(own[n, rows, :])
                    theirs.append(other[n, rows, :])
            x = jnp.concatenate(
                [jnp.concatenate(mine, axis=0), jnp.concatenate(theirs, axis=0)], axis=1
            )
            high = x.astype(bf16)
            low = (x - high.astype(f32)).astype(bf16)
            weight = wcat[j]
            contract = (((1,), (1,)), ((), ()))
            both = lax.dot_general(high, weight, contract, preferred_element_type=f32)
            rest = lax.dot_general(
                low, weight[0:ni], contract, preferred_element_type=f32
            )
            out = both[:, 0:ni] + (both[:, ni : 2 * ni] + rest)
            at = 0
            for n in range(cv):
                for k0 in starts:
                    smoothed[n, pl.ds(k0 * nj + j, count, stride=nj), :] = out[
                        at : at + count
                    ]
                    at += count

        return row

    def product(starts, count):
        row = row_product(starts, count)

        def one(j, carry):
            row(j)
            return carry

        lax.fori_loop(0, nj, one, 0, unroll=8)

    def update(first, number):
        def one(k, carry):
            rows = pl.ds(pl.multiple_of((first + k) * nj, nj), nj)
            scale = section_coefficient * tbuf[first + k]
            for n in range(cv):
                advanced[n, rows, :] = (
                    ubuf[n, first + k + 2, 8 : nj + 8, :] - scale * smoothed[n, rows, :]
                )
            return carry

        lax.fori_loop(0, number, one, 0, unroll=2)

    def arrived(n, carry):
        send(middle_pair(n)).wait_recv()
        return carry

    lax.fori_loop(0, pairs // 2, arrived, 0)
    middle_row = row_product([kl // 4], kl // 2)
    each = nj // (MIXED * PAIR)

    def run_mixed(n, carry):
        pair = outer_pair(n + 2 * (quarter - 1) - MIXED)

        def one(k, inner):
            for r in range(each):
                middle_row((n * PAIR + k) * each + r)
            plane(pair * PAIR + k)
            return inner

        lax.fori_loop(0, PAIR, one, 0)
        send(pair).start()
        return carry

    lax.fori_loop(0, MIXED, run_mixed, 0)
    update(kl // 4, kl // 2)

    to_right.wait()
    to_left.wait()

    for side, first in ((0, 0), (1, kl + 2)):
        turn = facing[side] == 1
        for p in range(2):
            for n in range(cv):
                at = (p * cv + n) * nj
                turned[0, at : at + nj, :] = ubuf[n, first + p, 8 : nj + 8, :]
        for j in range(nj):
            turned[1, pl.ds(j, 2 * cv, stride=nj), :] = turned[
                0, pl.ds(nj - 1 - j, 2 * cv, stride=nj), :
            ]
        for p in range(2):
            for n in range(cv):
                sign = -1.0 if n % nv == 2 else 1.0
                at = (p * cv + n) * nj
                ubuf[n, first + p, 8 : nj + 8, :] = jnp.where(
                    turn, sign * turned[1, at : at + nj, :], turned[0, at : at + nj, :]
                )

    work(0)
    work(pairs - 1)

    def outer_arrived(n, carry):
        send(outer_pair(n)).wait_recv()
        return carry

    lax.fori_loop(0, 2 * (quarter - 1), outer_arrived, 0)
    send(0).wait_recv()
    send(pairs - 1).wait_recv()
    product([0, kl - kl // 4], kl // 4)
    update(0, kl // 4)
    update(kl - kl // 4, kl // 4)

    def sent(pair, carry):
        send(pair).wait_send()
        return carry

    lax.fori_loop(0, pairs, sent, 0)


def write_out(advanced, smoothed, advanced_out, smoothed_out, sems):
    half = advanced.shape[0] // 2
    copies = []
    for n, (source, target) in enumerate(
        ((advanced, advanced_out), (smoothed, smoothed_out))
    ):
        for p in range(2):
            part = pl.ds(p * half, half)
            copies.append(
                pltpu.make_async_copy(
                    source.at[part], target.at[part], sems.at[2 * n + p]
                )
            )
    for copy in copies:
        copy.start()
    for copy in copies:
        copy.wait()


def body(
    nblk,
    base_state,
    gust_source,
    frequency,
    jacobians,
    dissipation,
    time_step,
    line_inverse,
    orientation,
):
    nc, nv, kl, nj, ni = base_state.shape
    cv = nc * nv
    f32 = jnp.float32
    pairs = kl // PAIR
    out = pltpu.VMEM((cv, kl * nj, ni), f32)
    smem = pl.BlockSpec(memory_space=pltpu.SMEM)
    hbm = pl.BlockSpec(memory_space=pltpu.HBM)
    vmem = pl.BlockSpec(memory_space=pltpu.VMEM)
    dma = pltpu.SemaphoreType.DMA
    advanced, smoothed = pl.pallas_call(
        functools.partial(kernel, (nblk, kl, nj, ni, cv)),
        out_shape=(out, out),
        in_specs=[smem] * 3 + [hbm] * 5,
        out_specs=(vmem, vmem),
        scratch_shapes=[
            pltpu.VMEM((cv, kl + 4, nj + 16, ni), f32),
            pltpu.VMEM((cv, kl, nj, ni), f32),
            pltpu.VMEM((kl, nj, ni), f32),
            pltpu.VMEM((kl, nj, ni), f32),
            pltpu.VMEM((nj, ni, 2 * ni), f32),
            pltpu.VMEM((nj, 2 * ni, 2 * ni), jnp.bfloat16),
            pltpu.VMEM((cv, nj, ni), f32),
            pltpu.VMEM((cv, nj, ni), f32),
            pltpu.VMEM((cv, kl * nj, ni), f32),
            pltpu.VMEM((cv, kl * nj, ni), f32),
            pltpu.VMEM((2, cv * 2 * nj, ni), f32),
            dma((6,)),
            dma((2,)),
            dma((2,)),
            dma,
            dma,
            dma((pairs,)),
            dma((pairs,)),
        ],
        compiler_params=pltpu.CompilerParams(
            collective_id=0, has_side_effects=True, vmem_limit_bytes=54 * 1024 * 1024
        ),
    )(
        jacobians.reshape(jacobians.shape[1:]),
        frequency,
        orientation.reshape(-1),
        base_state.reshape(cv, kl, nj, ni),
        gust_source.reshape(cv, kl, nj, ni),
        dissipation,
        time_step,
        line_inverse,
    )
    shape = jax.ShapeDtypeStruct((cv, kl * nj, ni), f32)
    advanced, smoothed = pl.pallas_call(
        write_out,
        out_shape=(shape, shape),
        in_specs=[vmem] * 2,
        out_specs=(hbm, hbm),
        scratch_shapes=[dma((4,))],
        compiler_params=pltpu.CompilerParams(vmem_limit_bytes=4 * 1024 * 1024),
    )(
        pltpu.with_memory_space_constraint(advanced, pltpu.VMEM),
        pltpu.with_memory_space_constraint(smoothed, pltpu.VMEM),
    )
    return advanced.reshape(base_state.shape), smoothed.reshape(base_state.shape)


def solution(mesh):
    in_specs = (
        P(None, None, ("freq", "blk"), None, "line"),
        P(None, None, ("freq", "blk"), None, "line"),
        P("freq"),
        P("blk", None, None, None),
        P("blk", None, "line"),
        P("blk", None, "line"),
        P(),
        P("blk", None),
    )
    out_specs = (
        P(None, None, ("freq", "blk"), None, "line"),
        P(None, None, ("freq", "blk"), None, "line"),
    )
    return jax.shard_map(
        functools.partial(body, mesh.shape["blk"]),
        mesh=mesh,
        in_specs=in_specs,
        out_specs=out_specs,
        check_vma=False,
    )
```

```python
import functools

import jax
import jax.numpy as jnp
from jax import lax
from jax.experimental import pallas as pl
from jax.experimental.pallas import tpu as pltpu
from jax.sharding import PartitionSpec as P

MESH = pl.DeviceIdType.MESH
section_coefficient = 0.25
PAIR = 2
MIXED = 4


def kernel(
    sizes,
    jac,
    freq,
    facing,
    base,
    gust,
    damp,
    step,
    inverse,
    smoothed,
    ubuf,
    tbuf,
    gbuf,
    dbuf,
    wbuf,
    wcat,
    pack_out,
    pack_in,
    own,
    other,
    turned,
    local_sem,
    halo_send,
    halo_recv,
    pack_send,
    pack_recv,
    res_send,
    res_recv,
):
    nblk, kl, nj, ni, cv = sizes
    nv = cv // 2
    f32, bf16 = jnp.float32, jnp.bfloat16
    blk = lax.axis_index("blk")
    line = lax.axis_index("line")
    right = lax.rem(blk + 1, nblk)
    left = lax.rem(blk + nblk - 1, nblk)
    mate = 1 - line

    loads = [
        pltpu.make_async_copy(
            base, ubuf.at[:, pl.ds(2, kl), pl.ds(8, nj), :], local_sem.at[0]
        ),
        pltpu.make_async_copy(
            inverse.at[:, pl.ds(pl.multiple_of(line * ni, ni), ni), pl.ds(pl.multiple_of(line * ni, ni), ni)],
            wbuf.at[:, :, pl.ds(0, ni)],
            local_sem.at[1],
        ),
        pltpu.make_async_copy(
            inverse.at[:, pl.ds(pl.multiple_of(line * ni, ni), ni), pl.ds(pl.multiple_of(mate * ni, ni), ni)],
            wbuf.at[:, :, pl.ds(ni, ni)],
            local_sem.at[2],
        ),
        pltpu.make_async_copy(gust, gbuf, local_sem.at[3]),
        pltpu.make_async_copy(damp, dbuf, local_sem.at[4]),
        pltpu.make_async_copy(step, tbuf, local_sem.at[5]),
    ]
    for copy in loads:
        copy.start()

    barrier = pltpu.get_barrier_semaphore()
    pl.semaphore_signal(barrier, inc=1, device_id={"blk": right}, device_id_type=MESH)
    pl.semaphore_signal(barrier, inc=1, device_id={"blk": left}, device_id_type=MESH)
    pl.semaphore_signal(barrier, inc=1, device_id={"line": mate}, device_id_type=MESH)
    pl.semaphore_wait(barrier, 3)

    to_right = pltpu.make_async_remote_copy(
        src_ref=base.at[:, pl.ds(kl - 2, 2)],
        dst_ref=ubuf.at[:, pl.ds(0, 2), pl.ds(8, nj), :],
        send_sem=halo_send.at[0],
        recv_sem=halo_recv.at[0],
        device_id={"blk": right},
        device_id_type=MESH,
    )
    to_left = pltpu.make_async_remote_copy(
        src_ref=base.at[:, pl.ds(0, 2)],
        dst_ref=ubuf.at[:, pl.ds(kl + 2, 2), pl.ds(8, nj), :],
        send_sem=halo_send.at[1],
        recv_sem=halo_recv.at[1],
        device_id={"blk": left},
        device_id_type=MESH,
    )
    to_right.start()
    to_left.start()

    def clear(k, carry):
        zero = jnp.zeros((cv, 8, ni), f32)
        ubuf[:, k + 2, 0:8, :] = zero
        ubuf[:, k + 2, nj + 8 : nj + 16, :] = zero
        return carry

    lax.fori_loop(0, kl, clear, 0)

    lane = lax.broadcasted_iota(jnp.int32, (nj, ni), 1)
    edge = (lane < 2) | (lane >= ni - 2)

    loads[0].wait()

    def pack(k, carry):
        return tuple(
            carry[n]
            + pltpu.roll(jnp.where(edge, ubuf[n, k + 2, 8 : nj + 8, :], 0.0), 4 * k, 1)
            for n in range(cv)
        )

    packed = lax.fori_loop(
        0, kl, pack, tuple(jnp.zeros((nj, ni), f32) for _ in range(cv)), unroll=8
    )
    for n in range(cv):
        pack_out[n] = packed[n]
    swap = pltpu.make_async_remote_copy(
        src_ref=pack_out,
        dst_ref=pack_in,
        send_sem=pack_send,
        recv_sem=pack_recv,
        device_id={"line": mate},
        device_id_type=MESH,
    )
    swap.start()

    loads[1].wait()
    loads[2].wait()

    def split(j, carry):
        values = wbuf[j]
        high = values.astype(bf16)
        wcat[j, 0:ni, :] = high
        wcat[j, ni : 2 * ni, :] = (values - high.astype(f32)).astype(bf16)
        return carry

    lax.fori_loop(0, nj, split, 0, unroll=2)

    loads[3].wait()
    loads[4].wait()
    loads[5].wait()
    swap.wait()

    omega = freq[0]

    def plane(k):
        damping = dbuf[k]
        shift = lax.rem(ni - 4 * k, ni)
        for c in range(2):
            central = []
            fourth = []
            for v in range(nv):
                n = c * nv + v
                u = ubuf[n, k + 2, 8 : nj + 8, :]
                k1, k2 = ubuf[n, k + 3, 8 : nj + 8, :], ubuf[n, k + 4, 8 : nj + 8, :]
                kb1, kb2 = ubuf[n, k + 1, 8 : nj + 8, :], ubuf[n, k, 8 : nj + 8, :]
                j1, j2 = ubuf[n, k + 2, 9 : nj + 9, :], ubuf[n, k + 2, 10 : nj + 10, :]
                jb1, jb2 = ubuf[n, k + 2, 7 : nj + 7, :], ubuf[n, k + 2, 6 : nj + 6, :]
                h = pltpu.roll(pack_in[n], shift, 1)
                i1 = pltpu.roll(jnp.where(lane == 0, h, u), ni - 1, 1)
                i2 = pltpu.roll(jnp.where(lane < 2, h, u), ni - 2, 1)
                ib1 = pltpu.roll(jnp.where(lane == ni - 1, h, u), 1, 1)
                ib2 = pltpu.roll(jnp.where(lane >= ni - 2, h, u), 2, 1)
                central.append((i1 - ib1, j1 - jb1, k1 - kb1))
                fourth.append(
                    ((k2 + kb2) + (j2 + jb2) + (i2 + ib2))
                    - 4.0 * ((k1 + kb1) + (j1 + jb1) + (i1 + ib1))
                    + 18.0 * u
                )
            for v in range(nv):
                flux = jnp.zeros((nj, ni), f32)
                for w in range(nv):
                    for d in range(3):
                        flux = flux + jac[d, v, w] * central[w][d]
                total = damping * fourth[v] - gbuf[c * nv + v, k] + 0.5 * flux
                if c == 0:
                    total = total - omega * ubuf[nv + v, k + 2, 8 : nj + 8, :]
                else:
                    total = total + omega * ubuf[v, k + 2, 8 : nj + 8, :]
                own[c * nv + v, pl.ds(pl.multiple_of(k * nj, nj), nj), :] = total

    def send(pair):
        rows = pl.ds(pl.multiple_of(pair * (PAIR * nj), PAIR * nj), PAIR * nj)
        return pltpu.make_async_remote_copy(
            src_ref=own.at[:, rows, :],
            dst_ref=other.at[:, rows, :],
            send_sem=res_send.at[pair],
            recv_sem=res_recv.at[pair],
            device_id={"line": mate},
            device_id_type=MESH,
        )

    def work(pair):
        def one(k, carry):
            plane(pair * PAIR + k)
            return carry

        lax.fori_loop(0, PAIR, one, 0)
        send(pair).start()

    pairs = kl // PAIR
    quarter = pairs // 4

    def middle_pair(n):
        return n + quarter

    def outer_pair(n):
        return n + 1 + (n // (quarter - 1)) * (pairs // 2)

    def run_middle(n, carry):
        work(middle_pair(n))
        return carry

    def run_outer(n, carry):
        work(outer_pair(n))
        return carry

    lax.fori_loop(0, pairs // 2, run_middle, 0)
    lax.fori_loop(0, 2 * (quarter - 1) - MIXED, run_outer, 0)

    def row_product(starts, count):
        def row(j):
            mine, theirs = [], []
            for n in range(cv):
                for k0 in starts:
                    rows = pl.ds(k0 * nj + j, count, stride=nj)
                    mine.append(own[n, rows, :])
                    theirs.append(other[n, rows, :])
            x = jnp.concatenate(
                [jnp.concatenate(mine, axis=0), jnp.concatenate(theirs, axis=0)], axis=1
            )
            high = x.astype(bf16)
            low = (x - high.astype(f32)).astype(bf16)
            weight = wcat[j]
            contract = (((1,), (1,)), ((), ()))
            both = lax.dot_general(high, weight, contract, preferred_element_type=f32)
            rest = lax.dot_general(
                low, weight[0:ni], contract, preferred_element_type=f32
            )
            out = both[:, 0:ni] + (both[:, ni : 2 * ni] + rest)
            at = 0
            for n in range(cv):
                for k0 in starts:
                    smoothed[n, pl.ds(k0 * nj + j, count, stride=nj), :] = out[
                        at : at + count
                    ]
                    at += count

        return row

    def product(starts, count):
        row = row_product(starts, count)

        def one(j, carry):
            row(j)
            return carry

        lax.fori_loop(0, nj, one, 0, unroll=16)

    def arrived(n, carry):
        send(middle_pair(n)).wait_recv()
        return carry

    lax.fori_loop(0, pairs // 2, arrived, 0)
    middle_row = row_product([kl // 4], kl // 2)
    each = nj // (MIXED * PAIR)

    def run_mixed(n, carry):
        pair = outer_pair(n + 2 * (quarter - 1) - MIXED)

        def one(k, inner):
            for r in range(each):
                middle_row((n * PAIR + k) * each + r)
            plane(pair * PAIR + k)
            return inner

        lax.fori_loop(0, PAIR, one, 0)
        send(pair).start()
        return carry

    lax.fori_loop(0, MIXED, run_mixed, 0)

    to_right.wait()
    to_left.wait()

    for side, first in ((0, 0), (1, kl + 2)):
        turn = facing[side] == 1
        for p in range(2):
            for n in range(cv):
                at = (p * cv + n) * nj
                turned[0, at : at + nj, :] = ubuf[n, first + p, 8 : nj + 8, :]
        for j in range(nj):
            turned[1, pl.ds(j, 2 * cv, stride=nj), :] = turned[
                0, pl.ds(nj - 1 - j, 2 * cv, stride=nj), :
            ]
        for p in range(2):
            for n in range(cv):
                sign = -1.0 if n % nv == 2 else 1.0
                at = (p * cv + n) * nj
                ubuf[n, first + p, 8 : nj + 8, :] = jnp.where(
                    turn, sign * turned[1, at : at + nj, :], turned[0, at : at + nj, :]
                )

    work(0)
    work(pairs - 1)

    def outer_arrived(n, carry):
        send(outer_pair(n)).wait_recv()
        return carry

    lax.fori_loop(0, 2 * (quarter - 1), outer_arrived, 0)
    send(0).wait_recv()
    send(pairs - 1).wait_recv()
    product([0, kl - kl // 4], kl // 4)

    def sent(pair, carry):
        send(pair).wait_send()
        return carry

    lax.fori_loop(0, pairs, sent, 0)


PARTS = 4


def write_out(smoothed, ubuf, tbuf, advanced_out, smoothed_out, abuf, sems):
    cv, rows_all, _ = smoothed.shape
    kl, nj, _ = tbuf.shape
    copies = []
    half = cv // 2
    for p in range(2):
        part = pl.ds(p * half, half)
        copies.append(
            pltpu.make_async_copy(smoothed.at[part], smoothed_out.at[part], sems.at[p])
        )
        copies[-1].start()
    planes = kl // PARTS
    for p in range(PARTS):

        def one(k, carry):
            rows = pl.ds(pl.multiple_of(k * nj, nj), nj)
            scale = section_coefficient * tbuf[k]
            for n in range(cv):
                abuf[n, rows, :] = (
                    ubuf[n, k + 2, 8 : nj + 8, :] - scale * smoothed[n, rows, :]
                )
            return carry

        lax.fori_loop(p * planes, (p + 1) * planes, one, 0, unroll=2)
        part = pl.ds(p * planes * nj, planes * nj)
        copies.append(
            pltpu.make_async_copy(
                abuf.at[:, part], advanced_out.at[:, part], sems.at[2 + p]
            )
        )
        copies[-1].start()
    for copy in copies:
        copy.wait()


def body(
    nblk,
    base_state,
    gust_source,
    frequency,
    jacobians,
    dissipation,
    time_step,
    line_inverse,
    orientation,
):
    nc, nv, kl, nj, ni = base_state.shape
    cv = nc * nv
    f32 = jnp.float32
    pairs = kl // PAIR
    out = pltpu.VMEM((cv, kl * nj, ni), f32)
    smem = pl.BlockSpec(memory_space=pltpu.SMEM)
    hbm = pl.BlockSpec(memory_space=pltpu.HBM)
    vmem = pl.BlockSpec(memory_space=pltpu.VMEM)
    dma = pltpu.SemaphoreType.DMA
    smoothed, ubuf, tbuf = pl.pallas_call(
        functools.partial(kernel, (nblk, kl, nj, ni, cv)),
        out_shape=(
            out,
            pltpu.VMEM((cv, kl + 4, nj + 16, ni), f32),
            pltpu.VMEM((kl, nj, ni), f32),
        ),
        in_specs=[smem] * 3 + [hbm] * 5,
        out_specs=(vmem,) * 3,
        scratch_shapes=[
            pltpu.VMEM((cv, kl, nj, ni), f32),
            pltpu.VMEM((kl, nj, ni), f32),
            pltpu.VMEM((nj, ni, 2 * ni), f32),
            pltpu.VMEM((nj, 2 * ni, 2 * ni), jnp.bfloat16),
            pltpu.VMEM((cv, nj, ni), f32),
            pltpu.VMEM((cv, nj, ni), f32),
            pltpu.VMEM((cv, kl * nj, ni), f32),
            pltpu.VMEM((cv, kl * nj, ni), f32),
            pltpu.VMEM((2, cv * 2 * nj, ni), f32),
            dma((6,)),
            dma((2,)),
            dma((2,)),
            dma,
            dma,
            dma((pairs,)),
            dma((pairs,)),
        ],
        compiler_params=pltpu.CompilerParams(
            collective_id=0, has_side_effects=True, vmem_limit_bytes=50 * 1024 * 1024
        ),
    )(
        jacobians.reshape(jacobians.shape[1:]),
        frequency,
        orientation.reshape(-1),
        base_state.reshape(cv, kl, nj, ni),
        gust_source.reshape(cv, kl, nj, ni),
        dissipation,
        time_step,
        line_inverse,
    )
    shape = jax.ShapeDtypeStruct((cv, kl * nj, ni), f32)
    advanced, smoothed = pl.pallas_call(
        write_out,
        out_shape=(shape, shape),
        in_specs=[vmem] * 3,
        out_specs=(hbm, hbm),
        scratch_shapes=[pltpu.VMEM((cv, kl * nj, ni), f32), dma((2 + PARTS,))],
        compiler_params=pltpu.CompilerParams(vmem_limit_bytes=4 * 1024 * 1024),
    )(
        pltpu.with_memory_space_constraint(smoothed, pltpu.VMEM),
        pltpu.with_memory_space_constraint(ubuf, pltpu.VMEM),
        pltpu.with_memory_space_constraint(tbuf, pltpu.VMEM),
    )
    return advanced.reshape(base_state.shape), smoothed.reshape(base_state.shape)


def solution(mesh):
    in_specs = (
        P(None, None, ("freq", "blk"), None, "line"),
        P(None, None, ("freq", "blk"), None, "line"),
        P("freq"),
        P("blk", None, None, None),
        P("blk", None, "line"),
        P("blk", None, "line"),
        P(),
        P("blk", None),
    )
    out_specs = (
        P(None, None, ("freq", "blk"), None, "line"),
        P(None, None, ("freq", "blk"), None, "line"),
    )
    return jax.shard_map(
        functools.partial(body, mesh.shape["blk"]),
        mesh=mesh,
        in_specs=in_specs,
        out_specs=out_specs,
        check_vma=False,
    )
```
